32 devices in a mesh: row: 8 (over y, x, core), col: 4 (over z).
Axes of the slice: x: 2, y: 2, z: 4, core: 2. Of those that a mesh axis runs over, the one named last changes fastest.
Arguments:
- objects: float32 [2, 2, 1024, 1024], P(None, None, 'row', 'col'), may hold values from -4 to 4
- illumination: float32 [2, 128, 128], replicated, may hold values from -4 to 4
- intensity: float32 [128, 128, 128], P(('row', 'col')), may hold values from 0 to 2
- row_offset: int32 [128], P(('row', 'col')), may hold values from 0 to 127
- col_offset: int32 [128], P(('row', 'col')), may hold values from 0 to 255
Outputs:
- object_grad: float32 [2, 2, 1024, 1024], P(None, None, 'row', 'col')
- probe_grad: float32 [2, 128, 128], replicated
The draws below stay inside these ranges and needn't reach their ends.
Inputs may be any that keep to these rules, and one draw needn't show every extreme that they name: `row_offset`: the row, within the tile of the device that holds position j, of the window's centre. `col_offset`: the column, within the tile of the device that holds position j, of the window's centre.
All inputs are finite; a program needn't handle non-finite values.
Results may differ from the reference program's by a relative error of at most 0.00013.
Values sent between devices are 32-bit elements; how exact they have to be, the bound alone decides.
No kernel may reach another device: no remote copies, remote signals or barrier semaphores. Data moves between devices by JAX's collectives and lax.ppermute only.
A program may use at most 64 MiB of HBM per device.

```python
import math
import jax
import jax.numpy as jnp
from jax import lax

PROBE = 128
TH = 128
TW = 256
POS_DEV = 4
NY = 1024
NX = 1024
NPOS = 128
N_ROW = 8
N_COL = 4


def with_ends(drawn, stream_key, smallest, high):
    extent = drawn.shape
    spot = [jax.random.randint(jax.random.fold_in(stream_key, axis), (), 0, extent[axis]) for axis in range(len(extent))]
    drawn = drawn.at[tuple(spot)].set(smallest)
    longest = extent.index(max(extent))
    spot[longest] = (spot[longest] + 1) % extent[longest]
    return drawn.at[tuple(spot)].set(high)


def block_scale(key, shape, shards, smallest, largest):
    gain = 1.0
    for dim, parts in shards:
        steps = jax.random.uniform(jax.random.fold_in(jax.random.fold_in(key, 6), dim), (parts,), jnp.float32, smallest / len(shards), largest / len(shards))
        gain = gain * jnp.repeat(jnp.exp(steps), shape[dim] // parts).reshape((-1,) + (1,) * (len(shape) - 1 - dim))
    return gain


def scatter_about(own_key, extent, width, limit, pieces=(), kind=jnp.bfloat16):
    drawn = width * jax.random.normal(own_key, extent, jnp.float32)
    if pieces:
        drawn = drawn * block_scale(own_key, extent, pieces, -0.22, 0.18)
    return jnp.clip(drawn, -limit, limit).astype(kind)


def setup_inputs(seed: int = 0) -> dict:
    key_of = jax.random.split(jax.random.key(seed), 6)
    objects = scatter_about(key_of[0], (2, 2, NY, NX), 0.7, 4.0, ((2, 8), (3, 4)), jnp.float32)
    illumination = scatter_about(key_of[1], (2, PROBE, PROBE), 0.7, 4.0, (), jnp.float32)
    intensity = jnp.clip(2.0 * jax.random.uniform(key_of[2], (NPOS, PROBE, PROBE), jnp.float32) ** block_scale(key_of[2], (NPOS, PROBE, PROBE), ((0, 32),), -0.2, 0.2), 0.0, 2.0)
    row_offset = with_ends(jax.random.randint(key_of[3], (NPOS,), 0, TH), jax.random.fold_in(key_of[3], 1), 0, TH - 1).astype(jnp.int32)
    col_offset = with_ends(jax.random.randint(key_of[4], (NPOS,), 0, TW), jax.random.fold_in(key_of[4], 1), 0, TW - 1).astype(jnp.int32)
    return dict(objects=objects, illumination=illumination, intensity=intensity, row_offset=row_offset, col_offset=col_offset)


depth = 0.5

def fresnel_phase(length):
    index = jnp.arange(length, dtype=jnp.int32)
    signed = jnp.where(index < length // 2, index, index - length)
    square = signed[:, None] ** 2 + signed[None, :] ** 2
    angle = -math.pi * depth / length * square.astype(jnp.float32)
    return (jnp.cos(angle), jnp.sin(angle))

def reference(objects, illumination, intensity, row_offset, col_offset):
    half_size = PROBE // 2
    cos_part, sin_part = fresnel_phase(PROBE)
    fresnel = lax.complex(cos_part, sin_part)
    object_field = lax.complex(objects[:, 0], objects[:, 1])
    padded = jnp.pad(object_field, ((0, 0), (half_size, half_size), (half_size, half_size)))
    probe_field = lax.complex(illumination[0], illumination[1])
    owner = jnp.arange(NPOS, dtype=jnp.int32) // POS_DEV
    row_start = (owner // N_COL * TH + row_offset).astype(jnp.int32)
    col_start = (owner % N_COL * TW + col_offset).astype(jnp.int32)
    anchor = jnp.zeros((), jnp.int32)

    def block_step(carry, first_index):
        total, probe_total = carry
        block_rows = lax.dynamic_slice_in_dim(row_start, first_index, POS_DEV)
        block_cols = lax.dynamic_slice_in_dim(col_start, first_index, POS_DEV)
        measured = lax.dynamic_slice_in_dim(intensity, first_index, POS_DEV, 0)

        def one_window(start_row, start_col):
            return lax.dynamic_slice(padded, (anchor, start_row, start_col), (2, PROBE, PROBE))
        windows = jax.vmap(one_window)(block_rows, block_cols)
        first_window = windows[:, 0]
        second_window = windows[:, 1]
        entry = probe_field * first_window
        moved = jnp.fft.ifft2(jnp.fft.fft2(entry, norm='ortho') * fresnel, norm='ortho')
        exit_wave = moved * second_window
        far_field = jnp.fft.fft2(exit_wave, norm='ortho')
        residual = jnp.real(far_field) ** 2 + jnp.imag(far_field) ** 2 - measured
        far_grad = residual * far_field
        exit_grad = jnp.fft.ifft2(far_grad, norm='ortho')
        moved_grad = jnp.conj(second_window) * exit_grad
        second_grad = jnp.conj(moved) * exit_grad
        entry_grad = jnp.fft.ifft2(jnp.fft.fft2(moved_grad, norm='ortho') * jnp.conj(fresnel), norm='ortho')
        first_grad = jnp.conj(probe_field) * entry_grad
        probe_total = probe_total + lax.optimization_barrier(jnp.sum(jnp.conj(first_window) * entry_grad, axis=0))
        stacked = jnp.stack([first_grad, second_grad], axis=1)

        def place(number, running):
            corner = (anchor, block_rows[number], block_cols[number])
            previous = lax.dynamic_slice(running, corner, (2, PROBE, PROBE))
            return lax.dynamic_update_slice(running, previous + stacked[number], corner)
        total = lax.fori_loop(0, POS_DEV, place, total)
        return ((total, probe_total), None)
    starts = jnp.arange(N_ROW * N_COL, dtype=jnp.int32) * POS_DEV
    initial = (jnp.zeros(padded.shape, padded.dtype), jnp.zeros((PROBE, PROBE), probe_field.dtype))
    (total, probe_total), unused = lax.scan(block_step, initial, starts)
    inner = total[:, half_size:half_size + NY, half_size:half_size + NX]
    object_grad = jnp.stack([jnp.real(inner), jnp.imag(inner)], axis=1)
    scaled = probe_total / math.sqrt(NPOS)
    probe_grad = jnp.stack([jnp.real(scaled), jnp.imag(scaled)])
    return (object_grad, probe_grad)
```

```python
import functools
import math

import jax
import jax.numpy as jnp
import ml_dtypes
import numpy as np
from jax import lax
from jax.experimental import pallas as pl
from jax.experimental.pallas import tpu as pltpu
from jax.sharding import PartitionSpec as P

depth = 0.5
LANES = 128
GROUP = 2


def split_host(values):
    high = values.astype(ml_dtypes.bfloat16)
    low = (values - high.astype(np.float64)).astype(ml_dtypes.bfloat16)
    return high, low


def operator_tables(length):
    index = np.arange(length)
    angle = -2.0 * math.pi / length * (index[:, None] * index[None, :] % length)
    fourier = np.exp(1j * angle) / math.sqrt(length)
    signed = np.where(index < length // 2, index, index - length)
    phase = np.exp(-1j * math.pi * depth / length * signed.astype(np.float64) ** 2)
    spread = np.conj(fourier) @ (phase[:, None] * fourier)
    spread = 0.5 * (spread + spread.T)
    tables = []
    for operator in (fourier, spread):
        real, imag = operator.real, operator.imag
        right = np.block([[real, imag], [-imag, real]])
        left = np.block([[real, -imag], [imag, real]])
        for block in (right, left):
            tables.extend(split_host(block))
    return np.stack(tables)


def split(values):
    high = values.astype(jnp.bfloat16)
    low = (values - high.astype(jnp.float32)).astype(jnp.bfloat16)
    return high, low


def dot(left, right):
    return jnp.dot(left, right, preferred_element_type=jnp.float32)


def halves(parity, length):
    near = pl.ds(pl.multiple_of(parity * length, length), length)
    far = pl.ds(pl.multiple_of((1 - parity) * length, length), length)
    return near, far


def side_strips(first, last, half):
    lane = lax.broadcasted_iota(jnp.int32, first[0].shape, 1)
    left = jnp.where(lane < half, first[0], pltpu.roll(first[1], half, 1))
    right = jnp.where(lane >= half, last[0], pltpu.roll(last[1], half, 1))
    return left, right


def kept(place, values):
    return jnp.where(place[0] >= 2, values, 0.0)


def pack_kernel(row_place, col_place, objects, row_cross, row_mate, col_cross, col_mate):
    half = row_cross.shape[1]
    outward, inward = halves(lax.rem(row_place[0], 2), half)
    even = lax.rem(col_place[0], 2) == 0
    for part in range(2):
        for comp in range(2):
            for tile in range(2):
                cols = slice(tile * LANES, (tile + 1) * LANES)
                row_cross[4 * part + 2 * comp + tile] = kept(
                    row_place, objects[part, comp, outward, cols]
                )
                row_mate[4 * part + 2 * comp + tile] = objects[part, comp, inward, cols]
        left, right = side_strips(
            (objects[part, 0, :, :LANES], objects[part, 1, :, :LANES]),
            (objects[part, 0, :, LANES:], objects[part, 1, :, LANES:]),
            half,
        )
        col_cross[part] = kept(col_place, jnp.where(even, left, right))
        col_mate[part] = jnp.where(even, right, left)


def corner_kernel(col_place, rows, ahead, col_mate, col_cross):
    half = rows.shape[1]
    even = lax.rem(col_place[0], 2) == 0
    for part in range(2):
        left, right = side_strips(
            (rows[4 * part], rows[4 * part + 2]),
            (rows[4 * part + 1], rows[4 * part + 3]),
            half,
        )
        col_cross[part] = kept(col_place, jnp.where(even, left, right))
        col_mate[part] = jnp.where(even, right, left)


def place_of(offsets, number):
    count = offsets.shape[0] // 2
    row = jnp.max(offsets[number : number + 1, :]).astype(jnp.int32)
    start = jnp.max(offsets[count + number : count + number + 1, :]).astype(jnp.int32)
    return row, start // LANES, lax.rem(start, LANES)


def outer_rows(row_place, beyond):
    half = LANES // 2
    outside = pl.ds(pl.multiple_of(row_place * beyond, half), half)
    inside = pl.ds(pl.multiple_of((1 - row_place) * beyond, half), half)
    return outside, inside


def turned(values, comp):
    return values if comp == 0 else pltpu.roll(values, LANES // 2, 1)


def prepare_kernel(
    row_far, col_far, objects_far, tables_far, probe_far, intensity_far,
    padded, tables, probe, intensity, offsets, row_offset, col_offset, arrived,
):
    half = LANES // 2
    height = objects_far.shape[2]
    pairs = [(row_far, row_offset), (col_far, col_offset)]
    for part in range(2):
        for comp in range(2):
            for tile in range(2):
                cols = slice(tile * LANES, (tile + 1) * LANES)
                pairs.append(
                    (
                        objects_far.at[part, comp, :, cols],
                        padded.at[2 * part + comp, 1 + tile, half : half + height],
                    )
                )
    pairs += [(tables_far, tables), (probe_far, probe), (intensity_far, intensity)]
    copies = [
        pltpu.make_async_copy(source, target, arrived.at[number])
        for number, (source, target) in enumerate(pairs)
    ]
    for copy in copies:
        copy.start()
    for copy in copies:
        copy.wait()
    count = offsets.shape[0] // 2
    for number in range(count):
        row = row_offset[number].astype(jnp.float32)
        start = (col_offset[number] + half).astype(jnp.float32)
        offsets[number] = jnp.full((LANES,), row, jnp.float32)
        offsets[count + number] = jnp.full((LANES,), start, jnp.float32)


def frame_kernel(
    row_place, col_place, row_cross, row_mate, col_mate, col_cross, padded_in, padded, *inner
):
    half = LANES // 2
    _, inward = halves(lax.rem(row_place[0], 2), half)
    near = jnp.concatenate(
        [strip[part, inward] for strip in (col_cross, col_mate) for part in range(2)]
    )
    start = 0
    for piece in inner:
        piece[...] = near[start : start + piece.shape[0]]
        start += piece.shape[0]
    height = col_mate.shape[1]
    outside, inside = outer_rows(lax.rem(row_place[0], 2), half + height)
    cross_tile = 3 * lax.rem(col_place[0], 2)
    mate_tile = 3 - cross_tile
    for part in range(2):
        for comp in range(2):
            ch = 2 * part + comp
            for tile in range(2):
                padded[ch, 1 + tile, outside] = row_cross[2 * ch + tile]
                padded[ch, 1 + tile, inside] = row_mate[2 * ch + tile]
            for tile, strip in ((cross_tile, col_cross), (mate_tile, col_mate)):
                padded[ch, tile, half : half + height] = turned(strip[part], comp)


def main_kernel(
    scale, row_place, col_place, tables, probe, intensity, offsets,
    corner_mate, corner_cross, inner_0, inner_1, inner_2, padded_in,
    padded, own, edge_cross, strip_cross, mate, side_cross, side_mate,
    probe_keep, probe_send, total,
):
    half = LANES // 2
    count = intensity.shape[0]
    lane = lax.broadcasted_iota(jnp.int32, (LANES, LANES), 1)
    outside, inside = outer_rows(lax.rem(row_place[0], 2), padded.shape[2] - half)
    cross_tile = 3 * lax.rem(col_place[0], 2)
    mate_tile = 3 - cross_tile
    inner = jnp.concatenate([inner_0[...], inner_1[...], inner_2[...]])
    for part in range(2):
        for comp in range(2):
            ch = 2 * part + comp
            for side, tile, corner in (
                (0, cross_tile, corner_cross),
                (1, mate_tile, corner_mate),
            ):
                padded[ch, tile, outside] = turned(corner[part], comp)
                at = (2 * side + part) * half
                padded[ch, tile, inside] = turned(inner[at : at + half], comp)
    places = [place_of(offsets, number) for number in range(count)]

    def window(number, ch):
        row, tile, shift = places[number]
        back = lax.rem(LANES - shift, LANES)
        first = pltpu.roll(padded[ch, tile, pl.ds(row, LANES), :], back, 1)
        second = pltpu.roll(padded[ch, tile + 1, pl.ds(row, LANES), :], back, 1)
        return jnp.where(lane < LANES - shift, first, second)

    def from_right(pairs, operator, conjugated):
        at = 4 * operator + (2 if conjugated else 0)
        entry = jnp.concatenate([jnp.concatenate(pair, axis=1) for pair in pairs], axis=0)
        high, low = split(entry)
        return dot(
            jnp.concatenate([high, low, high], axis=1),
            jnp.concatenate([tables[at], tables[at], tables[at + 1]], axis=0),
        )

    def from_left(middle, operator, conjugated):
        at = 4 * operator + (0 if conjugated else 2)
        members = middle.shape[0] // LANES
        stacked = jnp.concatenate(
            [
                jnp.concatenate(
                    [
                        middle[j * LANES : (j + 1) * LANES, c * LANES : (c + 1) * LANES]
                        for j in range(members)
                    ],
                    axis=1,
                )
                for c in range(2)
            ],
            axis=0,
        )
        high, low = split(stacked)
        final = dot(
            jnp.concatenate([tables[at], tables[at], tables[at + 1]], axis=1),
            jnp.concatenate([high, low, high], axis=0),
        )
        return [
            (
                final[:LANES, j * LANES : (j + 1) * LANES],
                final[LANES:, j * LANES : (j + 1) * LANES],
            )
            for j in range(members)
        ]

    def transform(groups, operator, conjugated):
        middles = [from_right(pairs, operator, conjugated) for pairs in groups]
        return [from_left(middle, operator, conjugated) for middle in middles]

    def times(left, right):
        return (left[0] * right[0] - left[1] * right[1], left[0] * right[1] + left[1] * right[0])

    def conj_times(left, right):
        return (left[0] * right[0] + left[1] * right[1], left[0] * right[1] - left[1] * right[0])

    illumination = (probe[0], probe[1])
    numbers = [
        list(range(first, min(first + GROUP, count))) for first in range(0, count, GROUP)
    ]
    w1 = [[(window(j, 0), window(j, 1)) for j in group] for group in numbers]
    moved = transform([[times(illumination, w) for w in group] for group in w1], 1, False)
    w2 = [[(window(j, 2), window(j, 3)) for j in group] for group in numbers]
    far = transform(
        [[times(b, w) for b, w in zip(*group)] for group in zip(moved, w2)], 0, False
    )
    far_grad = []
    for group, values in zip(numbers, far):
        far_grad.append([])
        for j, psi in zip(group, values):
            residual = psi[0] * psi[0] + psi[1] * psi[1] - intensity[j]
            far_grad[-1].append((residual * psi[0], residual * psi[1]))
    exit_grad = transform(far_grad, 0, True)
    moved_grad = [[conj_times(w, g) for w, g in zip(*group)] for group in zip(w2, exit_grad)]
    total[...] = jnp.zeros_like(total)

    def add(number, ch, values):
        row, tile, shift = places[number]
        rows = pl.ds(row, LANES)
        rolled = pltpu.roll(values, shift, 1)
        total[ch, tile, rows, :] += jnp.where(lane >= shift, rolled, 0.0)
        total[ch, tile + 1, rows, :] += jnp.where(lane < shift, rolled, 0.0)

    for group, waves, grads in zip(numbers, moved, exit_grad):
        for j, b, g in zip(group, waves, grads):
            second = conj_times(b, g)
            add(j, 2, second[0])
            add(j, 3, second[1])
    entry_grad = transform(moved_grad, 1, True)
    sums = None
    for windows, grads in zip(w1, entry_grad):
        for w, g in zip(windows, grads):
            term = conj_times(w, g)
            sums = term if sums is None else (sums[0] + term[0], sums[1] + term[1])
    upper = lax.rem(row_place[0], 2) == 0
    probe_keep[...] = scale * jnp.where(upper, sums[0], sums[1])
    probe_send[...] = scale * jnp.where(upper, sums[1], sums[0])
    for group, grads in zip(numbers, entry_grad):
        for j, g in zip(group, grads):
            first = conj_times(illumination, g)
            add(j, 0, first[0])
            add(j, 1, first[1])

    height = own.shape[2]
    even = lax.rem(col_place[0], 2) == 0
    for part in range(2):
        real, imag = 2 * part, 2 * part + 1
        for comp in range(2):
            ch = 2 * part + comp
            for tile in range(2):
                cols = slice(tile * LANES, (tile + 1) * LANES)
                own[part, comp, :, cols] = total[ch, 1 + tile, half : half + height]
                edge_cross[2 * ch + tile] = kept(row_place, total[ch, 1 + tile, outside])
                mate[2 * ch + tile] = total[ch, 1 + tile, inside]
        for rows, cross_at, mate_at in (
            (slice(half, half + height), (side_cross, part), (side_mate, part)),
            (outside, (strip_cross, part), (strip_cross, 2 + part)),
            (inside, (mate, 8 + part), (mate, 10 + part)),
        ):
            right, left = side_strips(
                (total[real, 3, rows], total[imag, 3, rows]),
                (total[real, 0, rows], total[imag, 0, rows]),
                half,
            )
            if rows is outside:
                left, right = kept(row_place, left), kept(row_place, right)
            cross_at[0][cross_at[1]] = jnp.where(even, left, right)
            mate_at[0][mate_at[1]] = jnp.where(even, right, left)


def sides_kernel(
    row_place, col_place, side_cross, side_mate, row_cross, row_mate, out_cross, out_mate
):
    near, far = halves(lax.rem(row_place[0], 2), row_cross.shape[1])
    for part in range(2):
        for rows, source, at in ((near, row_cross, part), (far, row_mate, 8 + part)):
            out_cross[part, rows] = kept(col_place, side_cross[part, rows] + source[at])
            out_mate[part, rows] = side_mate[part, rows] + source[at + 2]


def fold_kernel(
    row_place, col_place, own, row_cross, row_mate, col_mate, col_cross, out
):
    half = row_cross.shape[1]
    near, far = halves(lax.rem(row_place[0], 2), half)
    even = lax.rem(col_place[0], 2) == 0
    lane = lax.broadcasted_iota(jnp.int32, (half, LANES), 1)
    for part in range(2):
        for rows, source in ((near, row_cross), (far, row_mate)):
            cross = col_cross[part, rows]
            mate = col_mate[part, rows]
            left = jnp.where(even, cross, mate)
            right = jnp.where(even, mate, cross)
            for comp in range(2):
                ch = 2 * part + comp

                for tile in range(2):
                    cols = slice(tile * LANES, (tile + 1) * LANES)
                    if tile == 0:
                        side = jnp.where(lane < half, turned(left, comp), 0.0)
                    else:
                        side = jnp.where(lane >= half, turned(right, comp), 0.0)
                    out[part, comp, rows, cols] = (
                        own[part, comp, rows, cols] + side + source[2 * ch + tile]
                    )


def join_kernel(row_place, probe_half, probe_other, out):
    parity = lax.rem(row_place[0], 2)
    out[parity] = probe_half[...]
    out[1 - parity] = probe_other[...]


def add_kernel(left, right, out):
    out[...] = left[...] + right[...]


def local_call(
    kernel, out_shape, inputs, scalars=0, far=(), out_far=(), where=(), scratch=(),
    aliases=None, flops=0, size=1 << 20, vmem=6,
):
    near = pl.BlockSpec(memory_space=pltpu.VMEM)
    places = [
        pl.BlockSpec(memory_space=pltpu.SMEM)
        if number < scalars
        else pl.BlockSpec(memory_space=pltpu.HBM)
        if number in far
        else pl.BlockSpec(memory_space=pl.ANY)
        if number in where
        else near
        for number in range(len(inputs))
    ]
    shapes = [
        shape
        if isinstance(shape, jax.ShapeDtypeStruct)
        else jax.ShapeDtypeStruct(shape, jnp.float32)
        for shape in out_shape
    ]
    return pl.pallas_call(
        kernel,
        out_shape=shapes,
        in_specs=places,
        out_specs=[
            pl.BlockSpec(memory_space=pltpu.HBM) if number in out_far else near
            for number in range(len(out_shape))
        ],
        scratch_shapes=list(scratch),
        input_output_aliases=aliases or {},
        cost_estimate=pl.CostEstimate(flops=flops, bytes_accessed=size, transcendentals=0),
        compiler_params=pltpu.CompilerParams(vmem_limit_bytes=vmem << 20),
    )(*(
        pltpu.with_memory_space_constraint(value, pltpu.HBM) if number in far else value
        for number, value in enumerate(inputs)
    ))


def swap(values, axis, first, wrap=False):
    count = lax.axis_size(axis)
    partner = list(range(count))
    for i in range(first, count - 1, 2):
        partner[i], partner[i + 1] = i + 1, i
    if wrap:
        partner[0], partner[-1] = count - 1, 0
    return lax.ppermute(values, axis, list(enumerate(partner)))


def swap_inner_cols(values):
    rows, cols = lax.axis_size("row"), lax.axis_size("col")
    pairs = []
    for row in range(rows):
        for col in range(cols):
            to_row, to_col = row, col - 1 + 2 * (col % 2)
            if to_col < 0 or to_col >= cols:
                to_row, to_col = row + 1 - 2 * (row % 2), col
            pairs.append((row * cols + col, to_row * cols + to_col))
    return lax.ppermute(values, ("row", "col"), pairs)


def doubled(values, axis, bit):
    pairs = [(i, i ^ bit) for i in range(lax.axis_size(axis))]
    return added(values, lax.ppermute(values, axis, pairs))


def added(left, right):
    return local_call(add_kernel, [left.shape], [left, right])[0]


def on_device(objects, illumination, intensity, row_offset, col_offset):
    length = illumination.shape[-1]
    half = length // 2
    count = row_offset.shape[0]
    height, width = objects.shape[2:]
    tables = jnp.asarray(operator_tables(length))
    axes = ("row", "col")
    positions = count * lax.axis_size("row") * lax.axis_size("col")
    place = []
    for axis in axes:
        spot = lax.axis_index(axis).astype(jnp.int32)
        beyond = spot - 1 + 2 * lax.rem(spot, 2)
        inner = jnp.where((beyond >= 0) & (beyond < lax.axis_size(axis)), 2, 0)
        place.append((lax.rem(spot, 2) + inner).astype(jnp.int32).reshape(1))

    strip = (2, height, LANES)
    band = (8, half, LANES)
    corner = (4, half, LANES)
    field = (4, 4, height + 2 * half, LANES)
    row_cross, row_mate, col_cross, col_mate = local_call(
        pack_kernel,
        [band, band, strip, strip],
        [*place, objects],
        scalars=2,
    )
    row_cross = swap(row_cross, "row", 1, True)
    col_mate = swap(col_mate, "col", 0)
    col_cross = swap_inner_cols(col_cross)
    row_mate = swap(row_mate, "row", 0)
    padded, tables, probe, intensity, offsets = local_call(
        prepare_kernel,
        [
            field, jax.ShapeDtypeStruct(tables.shape, tables.dtype),
            illumination.shape, intensity.shape, (2 * count, LANES),
        ],
        [row_offset, col_offset, objects, tables, illumination, intensity],
        far=(0, 1, 2, 3, 4, 5),
        scratch=[
            pltpu.SMEM(row_offset.shape, jnp.int32),
            pltpu.SMEM(col_offset.shape, jnp.int32),
            pltpu.SemaphoreType.DMA((13,)),
        ],
        size=4 << 20,
        vmem=10,
    )
    corner_mate, corner_cross = local_call(
        corner_kernel,
        [(2, half, LANES), (2, half, LANES)],
        [place[1], row_cross, offsets],
        scalars=1,
        where=(2,),
    )
    corner_mate = swap(corner_mate, "col", 0)
    corner_cross = swap_inner_cols(corner_cross)
    third = -(-4 * half // 24) * 8
    padded, *inner = local_call(
        frame_kernel,
        [field, (third, LANES), (third, LANES), (4 * half - 2 * third, LANES)],
        [*place, row_cross, row_mate, col_mate, col_cross, padded],
        scalars=2,
        aliases={6: 0},
        vmem=10,
    )
    inner = [swap(piece, "row", 0) for piece in inner]
    (
        _, own, edge_cross, strip_cross, mate, side_cross, side_mate, probe_keep, probe_send,
    ) = local_call(
        functools.partial(main_kernel, 1.0 / math.sqrt(positions)),
        [
            field, objects.shape, band, corner, (12, half, LANES), strip, strip,
            (length, length), (length, length),
        ],
        [
            *place, tables, probe, intensity, offsets, corner_mate, corner_cross, *inner, padded,
        ],
        scalars=2,
        scratch=[pltpu.VMEM(field, jnp.float32)],
        aliases={11: 0},
        flops=3 * 2 * 256**3 * 16,
        size=8 << 20,
        vmem=18,
    )
    probe_half = added(probe_keep, swap(probe_send, "row", 0))
    for axis, bit in (("row", 2), ("col", 1)):
        while bit < lax.axis_size(axis):
            probe_half = doubled(probe_half, axis, bit)
            bit *= 2
    probe_other = swap(probe_half, "row", 0)
    strip_cross = swap(strip_cross, "row", 1, True)
    mate = swap(mate, "row", 0)
    edge_cross = swap(edge_cross, "row", 1, True)
    side_cross, side_mate = local_call(
        sides_kernel,
        [strip, strip],
        [*place, side_cross, side_mate, strip_cross, mate],
        scalars=2,
    )
    side_mate = swap(side_mate, "col", 0)
    side_cross = swap_inner_cols(side_cross)
    (object_grad,) = local_call(
        fold_kernel,
        [objects.shape],
        [*place, own, edge_cross, mate, side_mate, side_cross],
        scalars=2,
    )
    (probe_grad,) = local_call(
        join_kernel, [illumination.shape], [place[0], probe_half, probe_other], scalars=1
    )
    return (object_grad, probe_grad)


def solution(mesh):
    return jax.shard_map(
        on_device,
        mesh=mesh,
        in_specs=(
            P(None, None, "row", "col"),
            P(),
            P(("row", "col"), None, None),
            P(("row", "col")),
            P(("row", "col")),
        ),
        out_specs=(P(None, None, "row", "col"), P()),
        check_vma=False,
    )
```
